256 devices in a mesh: rep: 32 (over z_hi, x, core), tp: 8 (over z_lo, y).
Axes of the slice: x: 4, y: 4, z: 8 (z_hi: 4, z_lo: 2; z = z_hi * 2 + z_lo), core: 2. Of those that a mesh axis runs over, the one named last changes fastest.
Arguments:
- tokens: bfloat16 [32, 1024, 8192], P('rep'), may hold values from -6 to 6
- key_value_weight: bfloat16 [8192, 8, 2, 128], P(None, 'tp'), may hold values from -0.0625 to 0.0625
- replica_down_maps: float32 [32, 2, 16, 8192], P('rep'), may hold values from -6 to 6
- replica_up_maps: float32 [32, 16, 8, 2, 128], P('rep', None, 'tp'), may hold values from -6 to 6
- cotangent: bfloat16 [32, 1024, 8, 2, 128], P('rep', None, 'tp'), may hold values from -6 to 6
- optimizer_step_index: int32 [1], replicated, may hold values from 0 to 9999
Outputs:
- key_value_output: bfloat16 [32, 1024, 8, 2, 128], P('rep', None, 'tp')
- new_down: float32 [32, 2, 16, 8192], P('rep')
- new_up: float32 [32, 16, 8, 2, 128], P('rep', None, 'tp')
The draws below stay inside these ranges and needn't reach their ends.
All inputs are finite; a program needn't handle non-finite values.
Results may differ from the reference program's by a relative error of at most 0.0014.
The reference program's roundings to bfloat16 on the way (of `down_bf`, `up_bf`, `low_rank` and `grad_low`) count: a program that leaves them out, or rounds other values in their place, can miss the bound.
Values sent between devices are 32-bit elements; how exact they have to be, the bound alone decides.
No kernel may reach another device: no remote copies, remote signals or barrier semaphores. Data moves between devices by JAX's collectives and lax.ppermute only.
A program may use at most 128 MiB of HBM per device.

```python
import jax
import jax.numpy as jnp
from jax import lax

MODEL_DIM = 8192
KEY_VALUE_HEADS = 8
HEAD_DIM = 128
ADAPTER_RANK = 16
TOK = 1024
REPLICA_COUNT = 32
N_REP = 32


def level_of(own_key, dims, cuts, low, high):
    factor_of, own = 1.0, jax.random.fold_in(own_key, 6)
    for position, parts in cuts:
        draws = jnp.exp(jax.random.uniform(jax.random.fold_in(own, position), (parts,), jnp.float32, low / len(cuts), high / len(cuts)))
        factor_of = factor_of * jnp.repeat(draws, dims[position] // parts).reshape([-1 if axis == position else 1 for axis in range(len(dims))])
    return factor_of


def gaussian(rng, dims, scale, bound, cuts=(), kind=jnp.bfloat16):
    array = scale * jax.random.normal(rng, dims, jnp.float32)
    if cuts:
        array = array * level_of(rng, dims, cuts, -0.22, 0.18)
    return jnp.clip(array, -bound, bound).astype(kind)


def setup_inputs(seed: int = 0) -> dict:
    keys = jax.random.split(jax.random.key(seed), 7)
    return {
        "tokens": gaussian(keys[0], (REPLICA_COUNT, TOK, MODEL_DIM), 1.0, 6.0, ((0, 32),)),
        "key_value_weight": gaussian(keys[1], (MODEL_DIM, KEY_VALUE_HEADS, 2, HEAD_DIM), MODEL_DIM ** -0.5, 0.0625, ((1, 8),)),
        "replica_down_maps": gaussian(keys[2], (REPLICA_COUNT, 2, ADAPTER_RANK, MODEL_DIM), 1.0, 6.0, ((0, 32),), jnp.float32),
        "replica_up_maps": gaussian(keys[3], (REPLICA_COUNT, ADAPTER_RANK, KEY_VALUE_HEADS, 2, HEAD_DIM), 1.0, 6.0, ((0, 32), (2, 8)), jnp.float32),
        "cotangent": gaussian(keys[4], (REPLICA_COUNT, TOK, KEY_VALUE_HEADS, 2, HEAD_DIM), 1.0, 6.0, ((0, 32), (2, 8))),
        "optimizer_step_index": jax.random.randint(keys[5], (1,), 0, 10000).astype(jnp.int32),
    }


SCALE = 0.5


def reference(tokens, key_value_weight, replica_down_maps, replica_up_maps, cotangent, optimizer_step_index):
    flat_weight = key_value_weight.reshape(MODEL_DIM, KEY_VALUE_HEADS * 2 * HEAD_DIM)
    factor = MODEL_DIM ** -0.5
    step_value = optimizer_step_index[0].astype(jnp.float32)
    rate = 0.5 * (1.0 - 0.75 * step_value / 10000.0)

    def single_replica(items):
        inputs, down_adapter, up_adapter, grad_out = items
        down_bf = down_adapter.reshape(2 * ADAPTER_RANK, MODEL_DIM).astype(jnp.bfloat16)
        up_bf = up_adapter.astype(jnp.bfloat16)
        low_rank = (factor * jnp.dot(inputs, down_bf.T, preferred_element_type=jnp.float32)).astype(jnp.bfloat16)
        base = jnp.dot(inputs, flat_weight, preferred_element_type=jnp.float32).reshape(TOK, KEY_VALUE_HEADS, 2, HEAD_DIM)
        key_up = up_bf[:, :, 0, :].reshape(ADAPTER_RANK, KEY_VALUE_HEADS * HEAD_DIM)
        value_up = up_bf[:, :, 1, :].reshape(ADAPTER_RANK, KEY_VALUE_HEADS * HEAD_DIM)
        key_extra = jnp.dot(low_rank[:, :ADAPTER_RANK], key_up, preferred_element_type=jnp.float32)
        value_extra = jnp.dot(low_rank[:, ADAPTER_RANK:], value_up, preferred_element_type=jnp.float32)
        extra = jnp.stack([key_extra.reshape(TOK, KEY_VALUE_HEADS, HEAD_DIM), value_extra.reshape(TOK, KEY_VALUE_HEADS, HEAD_DIM)], axis=2)
        kv_block = (base + SCALE * extra).astype(jnp.bfloat16)
        key_grad = grad_out[:, :, 0, :].reshape(TOK, KEY_VALUE_HEADS * HEAD_DIM)
        value_grad = grad_out[:, :, 1, :].reshape(TOK, KEY_VALUE_HEADS * HEAD_DIM)
        back_low = jnp.concatenate([jnp.dot(key_grad, key_up.T, preferred_element_type=jnp.float32), jnp.dot(value_grad, value_up.T, preferred_element_type=jnp.float32)], axis=1)
        grad_low = (SCALE * back_low).astype(jnp.bfloat16)
        grad_down = factor * jnp.dot(grad_low.T, inputs, preferred_element_type=jnp.float32)
        grad_key_up = SCALE * jnp.dot(low_rank[:, :ADAPTER_RANK].T, key_grad, preferred_element_type=jnp.float32)
        grad_value_up = SCALE * jnp.dot(low_rank[:, ADAPTER_RANK:].T, value_grad, preferred_element_type=jnp.float32)
        grad_up = jnp.stack([grad_key_up.reshape(ADAPTER_RANK, KEY_VALUE_HEADS, HEAD_DIM), grad_value_up.reshape(ADAPTER_RANK, KEY_VALUE_HEADS, HEAD_DIM)], axis=2)
        shifted_down = down_adapter - rate * grad_down.reshape(2, ADAPTER_RANK, MODEL_DIM)
        shifted_up = up_adapter - rate * grad_up
        return kv_block, shifted_down, shifted_up

    key_value_output, shifted_down, shifted_up = lax.map(single_replica, (tokens, replica_down_maps, replica_up_maps, cotangent))
    bit_count = N_REP.bit_length() - 1
    shift_bit = jnp.mod(optimizer_step_index[0], bit_count).astype(jnp.int32)
    partner = jnp.bitwise_xor(jnp.arange(N_REP, dtype=jnp.int32), jnp.left_shift(jnp.int32(1), shift_bit))
    new_down = 0.5 * (shifted_down + jnp.take(shifted_down, partner, axis=0))
    new_up = 0.5 * (shifted_up + jnp.take(shifted_up, partner, axis=0))
    return key_value_output, new_down, new_up
```

```python
import jax
import jax.numpy as jnp
from jax import lax
from jax.sharding import PartitionSpec as P

SCALE = 0.5


def from_partner(value, axis, stride):
    mask = 2**stride
    pairs = [(source, source ^ mask) for source in range(lax.axis_size(axis))]
    return lax.ppermute(value, axis, pairs)


def swap_adapters(values, which_bit, bit_count):

    def branch_for(bit_number):
        return lambda payload: from_partner(payload, "rep", bit_number)

    return lax.switch(
        which_bit, [branch_for(bit_number) for bit_number in range(bit_count)], values
    )


def shards(
    tokens, key_value_weight, replica_down_maps, replica_up_maps, cotangent, optimizer_step_index
):
    tok_rows = tokens.shape[1]
    model_width = tokens.shape[2]
    adapter_rank_size = replica_up_maps.shape[1]
    local_heads = replica_up_maps.shape[2]
    head_dimension = replica_up_maps.shape[4]
    inputs = tokens[0]
    down_adapter = replica_down_maps[0]
    up_adapter = replica_up_maps[0]
    factor = model_width ** (-0.5)
    step_value = optimizer_step_index[0].astype(jnp.float32)
    rate = 0.5 * (1.0 - 0.75 * step_value / 10000.0)
    bit_count = lax.axis_size("rep").bit_length() - 1
    which_bit = optimizer_step_index[0] % bit_count
    flat_weight = key_value_weight.reshape(model_width, local_heads * 2 * head_dimension)
    down_bf = down_adapter.reshape(2 * adapter_rank_size, model_width).astype(jnp.bfloat16)
    up_bf = up_adapter.astype(jnp.bfloat16)
    low_rank = (
        factor
        * lax.dot_general(
            inputs, down_bf, (((1,), (1,)), ((), ())), preferred_element_type=jnp.float32
        )
    ).astype(jnp.bfloat16)
    base = jnp.dot(inputs, flat_weight, preferred_element_type=jnp.float32).reshape(
        tok_rows, local_heads, 2, head_dimension
    )
    key_up = up_bf[:, :, 0, :].reshape(adapter_rank_size, local_heads * head_dimension)
    value_up = up_bf[:, :, 1, :].reshape(adapter_rank_size, local_heads * head_dimension)
    key_extra = jnp.dot(low_rank[:, :adapter_rank_size], key_up, preferred_element_type=jnp.float32)
    value_extra = jnp.dot(
        low_rank[:, adapter_rank_size:], value_up, preferred_element_type=jnp.float32
    )
    extra = jnp.stack(
        [
            key_extra.reshape(tok_rows, local_heads, head_dimension),
            value_extra.reshape(tok_rows, local_heads, head_dimension),
        ],
        axis=2,
    )
    kv_block = (base + SCALE * extra).astype(jnp.bfloat16)
    grad_out = cotangent[0]
    key_grad = grad_out[:, :, 0, :].reshape(tok_rows, local_heads * head_dimension)
    value_grad = grad_out[:, :, 1, :].reshape(tok_rows, local_heads * head_dimension)
    contract_last = (((1,), (1,)), ((), ()))
    partial_low = jnp.concatenate(
        [
            lax.dot_general(key_grad, key_up, contract_last, preferred_element_type=jnp.float32),
            lax.dot_general(
                value_grad, value_up, contract_last, preferred_element_type=jnp.float32
            ),
        ],
        axis=1,
    )
    total_low = partial_low.T
    for mask in (4, 1, 3):
        pairs = [(source, source ^ mask) for source in range(lax.axis_size("tp"))]
        total_low = total_low + lax.ppermute(total_low, "tp", pairs)
    total_low = total_low.T
    grad_low = (SCALE * total_low).astype(jnp.bfloat16)
    contract_first = (((0,), (0,)), ((), ()))
    grad_down = (
        factor
        * lax.dot_general(grad_low, inputs, contract_first, preferred_element_type=jnp.float32)
    ).reshape(2, adapter_rank_size, model_width)
    grad_key_up = SCALE * lax.dot_general(
        low_rank[:, :adapter_rank_size],
        key_grad,
        contract_first,
        preferred_element_type=jnp.float32,
    )
    grad_value_up = SCALE * lax.dot_general(
        low_rank[:, adapter_rank_size:],
        value_grad,
        contract_first,
        preferred_element_type=jnp.float32,
    )
    grad_up = jnp.stack(
        [
            grad_key_up.reshape(adapter_rank_size, local_heads, head_dimension),
            grad_value_up.reshape(adapter_rank_size, local_heads, head_dimension),
        ],
        axis=2,
    )
    shifted_down = down_adapter - rate * grad_down
    shifted_up = up_adapter - rate * grad_up
    mate_down, mate_up = swap_adapters((shifted_down, shifted_up), which_bit, bit_count)
    mean_down = 0.5 * (shifted_down + mate_down)
    mean_up = 0.5 * (shifted_up + mate_up)
    return (kv_block[None], mean_down[None], mean_up[None])


def solution(mesh):
    placed = (
        P("rep", None, None),
        P(None, "tp", None, None),
        P("rep", None, None, None),
        P("rep", None, "tp", None, None),
        P("rep", None, "tp", None, None),
        P(),
    )
    return jax.shard_map(
        shards,
        mesh=mesh,
        in_specs=placed,
        out_specs=(
            P("rep", None, "tp", None, None),
            P("rep", None, None, None),
            P("rep", None, "tp", None, None),
        ),
        check_vma=False,
    )
```

```python
import functools

import jax
import jax.numpy as jnp
from jax import lax
from jax.experimental import pallas as pl
from jax.experimental.pallas import tpu as pltpu
from jax.sharding import PartitionSpec as P

SCALE = 0.5
PIECES = ((256, 512, 512, 512, 512, 512), (256, 512, 512, 512, 512, 512), (256, 512, 512, 512, 512, 256))
GRAD_BLOCK = 512
UP_COLUMNS = 128
NT = (((1,), (1,)), ((), ()))
HBM = pl.BlockSpec(memory_space=pltpu.HBM)
VMEM = pl.BlockSpec(memory_space=pltpu.VMEM)
SMEM = pl.BlockSpec(memory_space=pltpu.SMEM)


def params(mebibytes=40):
    return pltpu.CompilerParams(vmem_limit_bytes=mebibytes * 1024 * 1024)


def swap(value, axis, mask):
    pairs = [(source, source ^ mask) for source in range(lax.axis_size(axis))]
    return lax.ppermute(value, axis, pairs)


def rate_of(step_ref):
    step = jnp.full((1, 1), step_ref[0], jnp.int32).astype(jnp.float32)
    return 0.5 * (1.0 - 0.75 * step / 10000.0)


def every_other(ref, which, rows):
    return ref[pl.ds(which, rows, stride=2), :]


def low_grad_kernel(cot_hbm, up_hbm, low_ref, split_ref, cot_ref, up_ref, wide, sems):
    rank = up_ref.shape[0] // 2
    parts, part_rows = cot_ref.shape[:2]
    rows = part_rows // 2
    up_copy = pltpu.make_async_copy(up_hbm, up_ref, sems.at[parts])
    up_copy.start()
    copies = [
        pltpu.make_async_copy(
            cot_hbm.at[pl.ds(part * part_rows, part_rows)], cot_ref.at[part], sems.at[part]
        )
        for part in range(parts)
    ]
    for copy in copies:
        copy.start()
    up_copy.wait()
    ups = [every_other(up_ref, c, rank).astype(jnp.bfloat16) for c in range(2)]
    for part in range(parts):
        copies[part].wait()
        wide[...] = cot_ref[part].astype(jnp.float32)
        for c in range(2):
            cot = every_other(wide, c, rows).astype(jnp.bfloat16)
            split_ref[c, part * rows : (part + 1) * rows] = cot
            low_ref[c * rank : (c + 1) * rank, part * rows : (part + 1) * rows] = lax.dot_general(
                ups[c], cot, NT, preferred_element_type=jnp.float32
            )


def low_grad(cot, up):
    parts = 2
    rows, width = cot.shape[0] // 2, cot.shape[1]
    return pl.pallas_call(
        low_grad_kernel,
        in_specs=[HBM, HBM],
        out_specs=(VMEM, VMEM),
        out_shape=(
            jax.ShapeDtypeStruct((up.shape[0], rows), jnp.float32),
            jax.ShapeDtypeStruct((2, rows, width), jnp.bfloat16),
        ),
        scratch_shapes=[
            pltpu.VMEM((parts, 2 * rows // parts, width), jnp.bfloat16),
            pltpu.VMEM(up.shape, jnp.float32),
            pltpu.VMEM((2 * rows // parts, width), jnp.float32),
            pltpu.SemaphoreType.DMA((parts + 1,)),
        ],
        compiler_params=params(),
        name="low_grad",
    )(cot, up)


def accumulate(index, x_hbm, w_hbm, down_hbm, base, low, x_buf, w_buf, down_buf, wide, sems):
    first = sum(sum(piece) for piece in PIECES[:index])
    copies, at = [], 0
    for j, span in enumerate(PIECES[index]):
        sources = (
            x_hbm.at[:, pl.ds(first + at, span)],
            w_hbm.at[pl.ds(2 * (first + at), 2 * span)],
            down_hbm.at[:, pl.ds(first + at, span)],
        )
        targets = (
            x_buf.at[:, pl.ds(at, span)],
            w_buf.at[pl.ds(2 * at, 2 * span)],
            down_buf.at[:, pl.ds(at, span)],
        )
        copies.append(
            [
                pltpu.make_async_copy(source, target, sems.at[j, i])
                for i, (source, target) in enumerate(zip(sources, targets))
            ]
        )
        for copy in copies[-1]:
            copy.start()
        at += span
    at = 0
    for j, span in enumerate(PIECES[index]):
        for copy in copies[j]:
            copy.wait()
        x = x_buf[:, at : at + span]
        wide[: 2 * span] = w_buf[2 * at : 2 * (at + span)].astype(jnp.float32)
        weight = jnp.concatenate(
            [every_other(wide, c, span).astype(jnp.bfloat16) for c in range(2)], axis=1
        )
        down = down_buf[:, at : at + span].astype(jnp.bfloat16)
        base_part = jnp.dot(x, weight, preferred_element_type=jnp.float32)
        low_part = lax.dot_general(x, down, NT, preferred_element_type=jnp.float32)
        if index == 0 and j == 0:
            base[...] = base_part
            low[...] = low_part
        else:
            base[...] += base_part
            low[...] += low_part
        at += span


def first_kernel(x_hbm, w_hbm, down_hbm, base, low, *scratch):
    accumulate(0, x_hbm, w_hbm, down_hbm, base, low, *scratch)


def middle_kernel(index, x_hbm, w_hbm, down_hbm, base_in, low_in, base, low, *scratch):
    base[...] = base_in[...]
    low[...] = low_in[...]
    accumulate(index, x_hbm, w_hbm, down_hbm, base, low, *scratch)


def last_kernel(
    index, x_hbm, w_hbm, down_hbm, base_in, low_in, step_ref, up_ref, cot_ref,
    kv_ref, moved_ref, base, low, pair, *scratch,
):
    base[...] = base_in[...]
    low[...] = low_in[...]
    accumulate(index, x_hbm, w_hbm, down_hbm, base, low, *scratch)
    rows, width = cot_ref.shape[1:]
    rank = up_ref.shape[0] // 2
    factor = x_hbm.shape[1] ** (-0.5)
    low_rank = (factor * low[...]).astype(jnp.bfloat16)
    ups = [every_other(up_ref, c, rank) for c in range(2)]
    none = jnp.zeros((rank, width), jnp.float32)
    both = jnp.concatenate(
        [
            jnp.concatenate([ups[0], none], axis=1),
            jnp.concatenate([none, ups[1]], axis=1),
        ],
        axis=0,
    ).astype(jnp.bfloat16)
    extra = jnp.dot(low_rank, both, preferred_element_type=jnp.float32)
    kv = base[...] + SCALE * extra
    for c in range(2):
        pair[pl.ds(c, rows, stride=2), :] = kv[:, c * width : (c + 1) * width]
    kv_ref[...] = pair[...].astype(jnp.bfloat16)
    rate = rate_of(step_ref)
    turned = low_rank.T
    for c in range(2):
        grad = SCALE * jnp.dot(
            turned[c * rank : (c + 1) * rank], cot_ref[c], preferred_element_type=jnp.float32
        )
        moved_ref[c * rank : (c + 1) * rank, :] = ups[c] - rate * grad


def piece(index, x, weight, down, sums=(), last=()):
    rows = x.shape[0]
    width = weight.shape[1]
    ranks = down.shape[0]
    span = sum(PIECES[index])
    totals = [
        jax.ShapeDtypeStruct((rows, 2 * width), jnp.float32),
        jax.ShapeDtypeStruct((rows, ranks), jnp.float32),
    ]
    scratch = [
        pltpu.VMEM((rows, span), jnp.bfloat16),
        pltpu.VMEM((2 * span, width), jnp.bfloat16),
        pltpu.VMEM((ranks, span), jnp.float32),
        pltpu.VMEM((2 * max(PIECES[index]), width), jnp.float32),
        pltpu.SemaphoreType.DMA((len(PIECES[index]), 3)),
    ]
    in_specs = [HBM] * 3 + [VMEM] * len(sums)
    if index == 0:
        kernel = first_kernel
    elif not last:
        kernel = functools.partial(middle_kernel, index)
    outs = totals
    if last:
        kernel = functools.partial(last_kernel, index)
        in_specs += [SMEM, VMEM, VMEM]
        outs = [
            jax.ShapeDtypeStruct((2 * rows, width), jnp.bfloat16),
            jax.ShapeDtypeStruct(last[1].shape, jnp.float32),
        ]
        scratch = (
            [pltpu.VMEM(s.shape, s.dtype) for s in totals]
            + [pltpu.VMEM((2 * rows, width), jnp.float32)]
            + scratch
        )
    return pl.pallas_call(
        kernel,
        in_specs=in_specs,
        out_specs=[VMEM] * len(outs),
        out_shape=outs,
        scratch_shapes=scratch,
        compiler_params=params(),
        cost_estimate=pl.CostEstimate(
            flops=2 * rows * span * 4 * width,
            bytes_accessed=2 * span * (rows + 2 * width),
            transcendentals=0,
        ),
        name="piece",
    )(x, weight, down, *sums, *last)


def moved_kernel(span, first, with_up, x_hbm, down_hbm, here, there, step_ref, *refs):
    refs = list(refs)
    label_ref = refs.pop(0) if first is None else None
    up_ref = refs.pop(0) if with_up else None
    out, x_buf, down_buf, sems = refs
    begin = label_ref[0] * span if first is None else first
    blocks = span // GRAD_BLOCK
    copies = []
    for j in range(blocks):
        from_ = pl.ds(pl.multiple_of(begin + j * GRAD_BLOCK, GRAD_BLOCK), GRAD_BLOCK)
        to = pl.ds(j * GRAD_BLOCK, GRAD_BLOCK)
        copies.append(
            (
                pltpu.make_async_copy(x_hbm.at[:, from_], x_buf.at[:, to], sems.at[j, 0]),
                pltpu.make_async_copy(down_hbm.at[:, from_], down_buf.at[:, to], sems.at[j, 1]),
            )
        )
        for copy in copies[-1]:
            copy.start()
    factor = x_hbm.shape[1] ** (-0.5)
    rate = rate_of(step_ref)
    grad_low = (SCALE * (here[...] + there[...])).astype(jnp.bfloat16)
    if with_up:
        out[:, span:] = up_ref[...]
    for j in range(blocks):
        for copy in copies[j]:
            copy.wait()
        to = slice(j * GRAD_BLOCK, (j + 1) * GRAD_BLOCK)
        grad = factor * jnp.dot(grad_low, x_buf[:, to], preferred_element_type=jnp.float32)
        out[:, to] = down_buf[:, to] - rate * grad


def moved_columns(span, x, down, here, there, step, first=None, label=None, up=None):
    rows, ranks = x.shape[0], down.shape[0]
    extra = [(SMEM, label)] if first is None else []
    extra += [] if up is None else [(VMEM, up)]
    width = span + (0 if up is None else UP_COLUMNS)
    return pl.pallas_call(
        functools.partial(moved_kernel, span, first, up is not None),
        in_specs=[HBM, HBM, VMEM, VMEM, SMEM] + [spec for spec, _ in extra],
        out_specs=VMEM,
        out_shape=jax.ShapeDtypeStruct((ranks, width), jnp.float32),
        scratch_shapes=[
            pltpu.VMEM((rows, span), jnp.bfloat16),
            pltpu.VMEM((ranks, span), jnp.float32),
            pltpu.SemaphoreType.DMA((span // GRAD_BLOCK, 2)),
        ],
        compiler_params=params(),
        cost_estimate=pl.CostEstimate(
            flops=8 * rows * ranks * span, bytes_accessed=2 * rows * span, transcendentals=0
        ),
        name="moved",
    )(x, down, here, there, step, *[array for _, array in extra])


def store_up(here, there, new_up):
    rank = new_up.shape[0] // 2
    mean = 0.5 * (here + there)
    for c in range(2):
        new_up[pl.ds(c, rank, stride=2), :] = mean[c * rank : (c + 1) * rank]


def direct_kernel(here, there, new_down, new_up):
    span = new_down.shape[1]
    new_down[...] = 0.5 * (here[:, :span] + there[:, :span])
    store_up(here[:, span:], there[:, span:], new_up)


def gather_kernel(label_ref, here, there, own, from_z, from_y, from_side, new_down, new_up):
    span = own.shape[1]
    for mask, part in ((0, own), (3, from_z), (2, from_y), (1, from_side)):
        begin = pl.multiple_of((label_ref[0] ^ mask) * span, span)
        new_down[:, pl.ds(begin, span)] = part[...]
    width = new_down.shape[1] - 4 * span
    if width:
        new_down[:, 4 * span :] = 0.5 * (here[:, :width] + there[:, :width])
    at = here.shape[1] - UP_COLUMNS
    store_up(here[:, at:], there[:, at:], new_up)


def finish(kernel, specs, args, down, up):
    return pl.pallas_call(
        kernel,
        in_specs=specs,
        out_specs=(VMEM, VMEM),
        out_shape=(
            jax.ShapeDtypeStruct(down.shape, jnp.float32),
            jax.ShapeDtypeStruct(up.shape, jnp.float32),
        ),
        compiler_params=params(),
        name="finish",
    )(*args)


def direct(bit, x, down, here, there, step, label, up):
    moved = moved_columns(down.shape[1], x, down, here, there, step, first=0, up=up)
    return finish(direct_kernel, [VMEM] * 2, (moved, swap(moved, "rep", 1 << bit)), down, up)


def sliced(bit, span, x, down, here, there, step, label, up):
    rest = down.shape[1] - 4 * span
    if rest:
        moved = moved_columns(span, x, down, here, there, step, label=label)
        other = swap(moved, "rep", 1 << bit)
        later, _ = lax.optimization_barrier((here, moved))
        far = moved_columns(rest, x, down, later, there, step, first=4 * span, up=up)
        far_other = swap(far, "rep", 1 << bit)
        own = 0.5 * (moved + other)
    else:
        far = moved_columns(span, x, down, here, there, step, label=label, up=up)
        far_other = swap(far, "rep", 1 << bit)
        own = 0.5 * (far[:, :span] + far_other[:, :span])
    parts = [own] + [swap(own, "tp", mask) for mask in (4, 1, 3)]
    return finish(
        gather_kernel, [SMEM] + [VMEM] * 6, (label, far, far_other, *parts), down, up
    )


def shards(
    tokens, key_value_weight, replica_down_maps, replica_up_maps, cotangent, optimizer_step_index
):
    rows, depth = tokens.shape[1:]
    rank, _, _, width = replica_up_maps.shape[1:]
    x = tokens[0]
    weight = key_value_weight.reshape(2 * depth, width)
    down = replica_down_maps.reshape(2 * rank, depth)
    up = replica_up_maps.reshape(2 * rank, width)
    cot = cotangent.reshape(2 * rows, width)
    step = optimizer_step_index
    bit_count = lax.axis_size("rep").bit_length() - 1
    which_bit = step[0] % bit_count
    place = lax.axis_index("tp")
    z, y = place // 4, place % 4
    label = ((z ^ (y & 1) ^ (y >> 1)) * 2 + (z ^ (y >> 1))).astype(jnp.int32).reshape(1)

    low, split = low_grad(cot, up)
    from_z = swap(low, "tp", 4)
    sums = piece(0, x, weight, down)
    low = low + from_z
    from_y = swap(low, "tp", 1)
    sums = piece(1, x, weight, down, sums)
    low = low + from_y
    from_side = swap(low, "tp", 3)
    kv, moved_up = piece(2, x, weight, down, sums, (step, up, split))

    branches = [
        functools.partial(direct, 0),
        functools.partial(sliced, 1, 1024),
        functools.partial(sliced, 2, 1024),
        functools.partial(sliced, 3, 2048),
        functools.partial(sliced, 4, 2048),
    ][:bit_count]
    new_down, new_up = lax.switch(
        which_bit, branches, x, down, low, from_side, step, label, moved_up
    )
    return (
        kv.reshape(1, rows, 1, 2, width),
        new_down.reshape(replica_down_maps.shape),
        new_up.reshape(replica_up_maps.shape),
    )


def solution(mesh):
    placed = (
        P("rep", None, None),
        P(None, "tp", None, None),
        P("rep", None, None, None),
        P("rep", None, "tp", None, None),
        P("rep", None, "tp", None, None),
        P(),
    )
    return jax.shard_map(
        shards,
        mesh=mesh,
        in_specs=placed,
        out_specs=(
            P("rep", None, "tp", None, None),
            P("rep", None, None, None),
            P("rep", None, "tp", None, None),
        ),
        check_vma=False,
    )
```

```python
import functools

import jax
import jax.numpy as jnp
from jax import lax
from jax.experimental import pallas as pl
from jax.experimental.pallas import tpu as pltpu
from jax.sharding import PartitionSpec as P

SCALE = 0.5
PIECES = ((512,) * 5, (512,) * 5, (512,) * 6)
LATE = 0
AHEAD = (1, 1, 1)
GRAD_BLOCK = 512
SMALL_BLOCK = 256
WINDOW = 2048
HELD_WINDOWS = 1
UP_COLUMNS = 128
SPANS = (0, 1536, 1536, 2048, 2048)
FAR_FLOPS = 1
MEAN_FLOPS = 40_000_000_000
NT = (((1,), (1,)), ((), ()))
HBM = pl.BlockSpec(memory_space=pltpu.HBM)
VMEM = pl.BlockSpec(memory_space=pltpu.VMEM)
SMEM = pl.BlockSpec(memory_space=pltpu.SMEM)


def params(mebibytes=20):
    return pltpu.CompilerParams(vmem_limit_bytes=mebibytes * 1024 * 1024)


def swap(value, axis, mask):
    pairs = [(source, source ^ mask) for source in range(lax.axis_size(axis))]
    return lax.ppermute(value, axis, pairs)


def rate_of(step_ref):
    step = jnp.full((1, 1), step_ref[0], jnp.int32).astype(jnp.float32)
    return 0.5 * (1.0 - 0.75 * step / 10000.0)


def label_of(place_ref):
    place = place_ref[0]
    z, b = place >> 2, (place >> 1) & 1
    a = (place & 1) ^ b
    return (z ^ a) * 2 + (z ^ b)


def every_other(ref, which, rows):
    return ref[pl.ds(which, rows, stride=2), :]


def in_hbm(*arrays):
    return [pltpu.with_memory_space_constraint(array, pltpu.HBM) for array in arrays]


def columns(ref, first, span):
    return ref.at[:, pl.ds(first, span)]


def span_copies(stored, targets, first, span, sems):
    x, weight, down = stored
    sources = (
        columns(x, first, span),
        None if weight is None else weight.at[pl.ds(2 * first, 2 * span)],
        None if down is None else columns(down, first, span),
    )
    return [
        pltpu.make_async_copy(source, target, sems.at[i])
        for i, (source, target) in enumerate(zip(sources, targets))
        if source is not None
    ]


def start_all(copies):
    for copy in copies:
        copy.start()


def wait_all(copies):
    for copy in copies:
        copy.wait()


def low_grad_kernel(
    cot_hbm, up_hbm, x_hbm, w_hbm, down_hbm,
    low_ref, split_ref, x_ref, w_ref, down_ref, cot_ref, up_ref, wide, sems, ahead_sems,
):
    rank = up_ref.shape[0] // 2
    parts, part_rows = cot_ref.shape[:2]
    rows = part_rows // 2
    up_copy = pltpu.make_async_copy(up_hbm, up_ref, sems.at[parts])
    copies = [
        pltpu.make_async_copy(
            cot_hbm.at[pl.ds(part * part_rows, part_rows)], cot_ref.at[part], sems.at[part]
        )
        for part in range(parts)
    ]
    start_all([up_copy, *copies])
    span = x_ref.shape[1]
    ahead = span_copies((x_hbm, w_hbm, down_hbm), (x_ref, w_ref, down_ref), 0, span, ahead_sems)
    start_all(ahead)
    up_copy.wait()
    ups = [every_other(up_ref, c, rank).astype(jnp.bfloat16) for c in range(2)]
    for part in range(parts):
        copies[part].wait()
        wide[...] = cot_ref[part].astype(jnp.float32)
        for c in range(2):
            cot = every_other(wide, c, rows).astype(jnp.bfloat16)
            split_ref[c, part * rows : (part + 1) * rows] = cot
            low_ref[c * rank : (c + 1) * rank, part * rows : (part + 1) * rows] = lax.dot_general(
                ups[c], cot, NT, preferred_element_type=jnp.float32
            )
    wait_all(ahead)


def ahead_span(index):
    return sum(PIECES[index][: AHEAD[index]])


def ahead_shapes(index, x, weight, down):
    span = ahead_span(index)
    return [
        jax.ShapeDtypeStruct((x.shape[0], span), x.dtype),
        jax.ShapeDtypeStruct((2 * span, weight.shape[1]), weight.dtype),
        jax.ShapeDtypeStruct((down.shape[0], span), down.dtype),
    ]


def low_grad(cot, up, x, weight, down):
    parts = 2
    rows, width = cot.shape[0] // 2, cot.shape[1]
    return pl.pallas_call(
        low_grad_kernel,
        in_specs=[HBM] * 5,
        out_specs=[VMEM] * 5,
        out_shape=(
            jax.ShapeDtypeStruct((up.shape[0], rows), jnp.float32),
            jax.ShapeDtypeStruct((2, rows, width), jnp.bfloat16),
            *ahead_shapes(0, x, weight, down),
        ),
        scratch_shapes=[
            pltpu.VMEM((parts, 2 * rows // parts, width), jnp.bfloat16),
            pltpu.VMEM(up.shape, jnp.float32),
            pltpu.VMEM((2 * rows // parts, width), jnp.float32),
            pltpu.SemaphoreType.DMA((parts + 1,)),
            pltpu.SemaphoreType.DMA((3,)),
        ],
        compiler_params=params(),
        name="low_grad",
    )(*in_hbm(cot, up, x, weight, down))


def accumulate(index, stored, held, base, low, buffers, sems):
    x_buf, w_buf, down_buf, wide = buffers
    begin, at, skipped = sum(sum(piece) for piece in PIECES[:index]), 0, 0
    late = len(PIECES[index]) - (LATE if index == len(PIECES) - 1 else 0)
    work = []
    for j, span in enumerate(PIECES[index]):
        ahead = held is not None and j < AHEAD[index]
        if low is None and j < late or ahead:
            skipped += span
        x_ref, w_ref, down_ref = held if ahead else (x_buf, w_buf, down_buf)
        here = at if ahead else at - skipped
        with_base = base is not None and (low is None or j < late)
        targets = (
            columns(x_ref, here, span),
            w_ref.at[pl.ds(2 * here, 2 * span)] if with_base else None,
            None if low is None else columns(down_ref, here, span),
        )
        x, weight, down = stored
        needed = (x, weight if with_base else None, down)
        if low is not None or j >= late:
            copies = [] if ahead else span_copies(needed, targets, begin + at, span, sems.at[j])
            start_all(copies)
            work.append((span, with_base, copies, targets))
        at += span

    def compute():
        for j, (span, with_base, copies, (x_ref, w_ref, down_ref)) in enumerate(work):
            wait_all(copies)
            x = x_ref[...]
            clear = index == 0 and j == 0
            if with_base:
                wide[: 2 * span] = w_ref[...].astype(jnp.float32)
                weight = jnp.concatenate(
                    [every_other(wide, c, span).astype(jnp.bfloat16) for c in range(2)], axis=1
                )
                base_part = jnp.dot(x, weight, preferred_element_type=jnp.float32)
                base[...] = base_part if clear else base[...] + base_part
            if low is not None:
                down = down_ref[...].astype(jnp.bfloat16)
                low_part = lax.dot_general(down, x, NT, preferred_element_type=jnp.float32)
                low[...] = low_part if clear else low[...] + low_part

    return begin + at, compute


def piece_kernel(index, *refs):
    stored, held, refs = refs[:3], refs[3:6], refs[6 if index == 0 else 8 :]
    base, low, *refs = refs
    targets, buffers, sems = refs[:3], refs[3:7], refs[7]
    end, compute = accumulate(index, stored, held, base, low, buffers, sems)
    ahead = span_copies(stored, targets, end, ahead_span(index + 1), sems.at[0])
    start_all(ahead)
    compute()
    wait_all(ahead)


def last_kernel(index, *refs):
    stored, held, refs = refs[:3], refs[3:6], refs[6:]
    _, low_in, place_ref, step_ref, up_ref, cot_ref, *refs = refs
    base, moved_ref, turned_ref, x_window, down_window, low, *buffers, sems = refs
    _, compute = accumulate(index, stored, held, base, low, buffers, sems)
    x_hbm, _, down_hbm = stored
    windows = x_hbm.shape[1] // WINDOW
    held_windows = []
    for n in range(HELD_WINDOWS):
        begin = pl.multiple_of(lax.rem(label_of(place_ref) + n, windows) * WINDOW, WINDOW)
        for i, (source, target) in enumerate(((x_hbm, x_window), (down_hbm, down_window))):
            copy = pltpu.make_async_copy(
                columns(source, begin, WINDOW),
                columns(target, n * WINDOW, WINDOW),
                sems.at[len(PIECES[index]) + n, i],
            )
            copy.start()
            held_windows.append(copy)
    low[...] = low_in[...]
    compute()
    rank = up_ref.shape[0] // 2
    factor = x_hbm.shape[1] ** (-0.5)
    turned = (factor * low[...]).astype(jnp.bfloat16)
    turned_ref[...] = turned
    rate = rate_of(step_ref)
    for c in range(2):
        grad = SCALE * jnp.dot(
            turned[c * rank : (c + 1) * rank], cot_ref[c], preferred_element_type=jnp.float32
        )
        moved_ref[c * rank : (c + 1) * rank, :] = every_other(up_ref, c, rank) - rate * grad
    wait_all(held_windows)


def kv_kernel(index, x_hbm, w_hbm, base_in, turned_ref, up_ref, kv_ref, base, pair, *refs):
    x_buf, w_buf, wide, out, sems = refs
    _, compute = accumulate(
        index, (x_hbm, w_hbm, None), None, base, None, (x_buf, w_buf, None, wide), sems
    )
    rows, width = kv_ref.shape[0] // 2, kv_ref.shape[1]
    rank = up_ref.shape[0] // 2
    ups = [every_other(up_ref, c, rank) for c in range(2)]
    none = jnp.zeros((rank, width), jnp.float32)
    both = jnp.concatenate(
        [
            jnp.concatenate([ups[0], none], axis=1),
            jnp.concatenate([none, ups[1]], axis=1),
        ],
        axis=0,
    ).astype(jnp.bfloat16)
    extra = jnp.dot(turned_ref[...].T, both, preferred_element_type=jnp.float32)
    base[...] = base_in[...] + SCALE * extra
    if LATE:
        compute()
    for c in range(2):
        pair[pl.ds(c, rows, stride=2), :] = base[:, c * width : (c + 1) * width]
    out[...] = pair[...].astype(jnp.bfloat16)
    copy = pltpu.make_async_copy(out, kv_ref, sems.at[0, 0])
    copy.start()
    copy.wait()


def key_values(x, weight, base, turned, up):
    rows, width = x.shape[0], weight.shape[1]
    index = len(PIECES) - 1
    span = max(sum(PIECES[index][len(PIECES[index]) - LATE :]), 128)
    return pl.pallas_call(
        functools.partial(kv_kernel, index),
        in_specs=[HBM] * 2 + [VMEM] * 3,
        out_specs=HBM,
        out_shape=pltpu.HBM((2 * rows, width), jnp.bfloat16),
        scratch_shapes=[
            pltpu.VMEM(base.shape, base.dtype),
            pltpu.VMEM((2 * rows, width), jnp.float32),
            pltpu.VMEM((rows, span), x.dtype),
            pltpu.VMEM((2 * span, width), weight.dtype),
            pltpu.VMEM((2 * max(PIECES[index]), width), jnp.float32),
            pltpu.VMEM((2 * rows, width), jnp.bfloat16),
            pltpu.SemaphoreType.DMA((len(PIECES[index]), 3)),
        ],
        compiler_params=params(),
        cost_estimate=pl.CostEstimate(
            flops=2 * rows * span * 4 * width, bytes_accessed=2 * span * (rows + 2 * width), transcendentals=0
        ),
        name="key_values",
    )(*in_hbm(x, weight), base, turned, up)


def last_piece(index, stored, held, sums, last):
    x, weight, down = stored
    base, low = sums
    rows, width, ranks = x.shape[0], weight.shape[1], down.shape[0]
    span = sum(PIECES[index])
    rest = span - ahead_span(index)
    return pl.pallas_call(
        functools.partial(last_kernel, index),
        in_specs=[HBM] * 3 + [VMEM] * 5 + [SMEM, SMEM, VMEM, VMEM],
        out_specs=[VMEM] * 5,
        input_output_aliases={6: 0},
        out_shape=[
            jax.ShapeDtypeStruct(base.shape, base.dtype),
            jax.ShapeDtypeStruct(last[2].shape, jnp.float32),
            jax.ShapeDtypeStruct(low.shape, jnp.bfloat16),
            jax.ShapeDtypeStruct((rows, HELD_WINDOWS * WINDOW), x.dtype),
            jax.ShapeDtypeStruct((ranks, HELD_WINDOWS * WINDOW), down.dtype),
        ],
        scratch_shapes=[
            pltpu.VMEM(low.shape, low.dtype),
            pltpu.VMEM((rows, rest), x.dtype),
            pltpu.VMEM((2 * rest, width), weight.dtype),
            pltpu.VMEM((ranks, rest), down.dtype),
            pltpu.VMEM((2 * max(PIECES[index]), width), jnp.float32),
            pltpu.SemaphoreType.DMA((len(PIECES[index]) + HELD_WINDOWS, 3)),
        ],
        compiler_params=params(),
        cost_estimate=pl.CostEstimate(
            flops=2 * rows * span * 512, bytes_accessed=2 * span * rows, transcendentals=0
        ),
        name="last_piece",
    )(*in_hbm(*stored), *held, *sums, *last)


def piece(index, stored, held, sums=()):
    x, weight, down = stored
    rows, width, ranks = x.shape[0], weight.shape[1], down.shape[0]
    totals = [
        jax.ShapeDtypeStruct((rows, 2 * width), jnp.float32),
        jax.ShapeDtypeStruct((ranks, rows), jnp.float32),
    ]
    span = sum(PIECES[index])
    rest = span - ahead_span(index)
    scratch = [
        pltpu.VMEM((rows, rest), x.dtype),
        pltpu.VMEM((2 * rest, width), weight.dtype),
        pltpu.VMEM((ranks, rest), down.dtype),
        pltpu.VMEM((2 * max(PIECES[index]), width), jnp.float32),
        pltpu.SemaphoreType.DMA((len(PIECES[index]), 3)),
    ]
    in_specs = [HBM] * 3 + [VMEM] * (3 + len(sums))
    kernel = functools.partial(piece_kernel, index)
    outs = totals + ahead_shapes(index + 1, *stored)
    aliases = {6: 0, 7: 1} if sums else {}
    out = pl.pallas_call(
        kernel,
        in_specs=in_specs,
        out_specs=[VMEM] * len(outs),
        out_shape=outs,
        scratch_shapes=scratch,
        input_output_aliases=aliases,
        compiler_params=params(),
        cost_estimate=pl.CostEstimate(
            flops=2 * rows * span * 4 * width,
            bytes_accessed=2 * span * (rows + 2 * width),
            transcendentals=0,
        ),
        name="piece",
    )(*in_hbm(*stored), *held, *sums)
    return out[2:], out[:2]


def moved_kernel(at, span, others, with_up, *refs):
    refs = list(refs)
    x_window, down_window, here, there, step_ref = refs[:5]
    refs = refs[5:]
    up_ref = refs.pop(0) if with_up else None
    block = GRAD_BLOCK if span % GRAD_BLOCK == 0 else SMALL_BLOCK
    work = [
        (columns(x_window, n * WINDOW + at, span), columns(down_window, n * WINDOW + at, span), ())
        for n in range(HELD_WINDOWS if others else 1)
    ]
    if others:
        place_ref, x_hbm, down_hbm, out, x_buf, down_buf, sems = refs
        windows = x_hbm.shape[1] // WINDOW
        for i in range(HELD_WINDOWS, windows):
            window = lax.rem(label_of(place_ref) + i, windows)
            for j in range(span // block):
                n = (i - HELD_WINDOWS) * (span // block) + j
                source = pl.multiple_of(window * WINDOW + at + j * block, block)
                targets = [columns(buf, n * block, block) for buf in (x_buf, down_buf)]
                copies = [
                    pltpu.make_async_copy(columns(x_hbm, source, block), targets[0], sems.at[n, 0]),
                    pltpu.make_async_copy(columns(down_hbm, source, block), targets[1], sems.at[n, 1]),
                ]
                start_all(copies)
                work.append((*targets, copies))
    else:
        (out,) = refs
    factor = (4 * WINDOW) ** (-0.5)
    rate = rate_of(step_ref)
    grad_low = (SCALE * (here[...] + there[...])).astype(jnp.bfloat16)
    place = 0
    for x_ref, down_ref, copies in work:
        wait_all(copies)
        grad = factor * jnp.dot(grad_low, x_ref[...], preferred_element_type=jnp.float32)
        width = x_ref.shape[1]
        out[:, place : place + width] = down_ref[...] - rate * grad
        place += width
    if with_up:
        out[:, place:] = up_ref[...]


def moved_columns(window, sums, at, span, stored=(), up=None, flops=1):
    (x, down), (here, there, step) = window, sums
    rows, ranks = x.shape[0], down.shape[0]
    block = GRAD_BLOCK if span % GRAD_BLOCK == 0 else SMALL_BLOCK
    in_specs, args = [VMEM] * 4 + [SMEM], [x, down, here, there, step]
    if up is not None:
        in_specs += [VMEM]
        args += [up]
    scratch, total = [], span
    if stored:
        place, x_all, down_all = stored
        total = span * (x_all.shape[1] // WINDOW)
        in_specs += [SMEM, HBM, HBM]
        args += [place, *in_hbm(x_all, down_all)]
        rest = total - HELD_WINDOWS * span
        scratch = [
            pltpu.VMEM((rows, rest), x.dtype),
            pltpu.VMEM((ranks, rest), down.dtype),
            pltpu.SemaphoreType.DMA((rest // block, 2)),
        ]
    return pl.pallas_call(
        functools.partial(moved_kernel, at, span, bool(stored), up is not None),
        in_specs=in_specs,
        out_specs=VMEM,
        out_shape=jax.ShapeDtypeStruct((ranks, total + (0 if up is None else UP_COLUMNS)), jnp.float32),
        scratch_shapes=scratch,
        compiler_params=params(),
        cost_estimate=pl.CostEstimate(
            flops=8 * rows * ranks * total * flops, bytes_accessed=2 * rows * total, transcendentals=0
        ),
        name="moved",
    )(*args)


def store_up(here, there, new_up):
    rank = new_up.shape[0] // 2
    mean = 0.5 * (here + there)
    for c in range(2):
        new_up[pl.ds(c, rank, stride=2), :] = mean[c * rank : (c + 1) * rank]


def store_others(place_ref, here, there, at, span, new_down):
    windows = new_down.shape[1] // WINDOW
    for i in range(windows):
        window = lax.rem(label_of(place_ref) + i, windows)
        begin = pl.multiple_of(window * WINDOW + at, SMALL_BLOCK)
        part = slice(i * span, (i + 1) * span)
        new_down[:, pl.ds(begin, span)] = 0.5 * (here[:, part] + there[:, part])


def direct_kernel(place_ref, here, there, new_down, new_up):
    store_others(place_ref, here, there, 0, WINDOW, new_down)
    span = new_down.shape[1]
    store_up(here[:, span:], there[:, span:], new_up)


def gather_kernel(place_ref, here, there, own, from_z, from_y, from_side, new_down, new_up):
    span = own.shape[1]
    for mask, part in ((0, own), (3, from_z), (2, from_y), (1, from_side)):
        begin = pl.multiple_of((label_of(place_ref) ^ mask) * WINDOW, WINDOW)
        new_down[:, pl.ds(begin, span)] = part[...]
    if span < WINDOW:
        store_others(place_ref, here, there, span, WINDOW - span, new_down)
    at = here.shape[1] - UP_COLUMNS
    store_up(here[:, at:], there[:, at:], new_up)


def mean_kernel(here, there, mean):
    span = mean.shape[1]
    mean[...] = 0.5 * (here[:, :span] + there[:, :span])


def mean_of(here, there, span):
    return pl.pallas_call(
        mean_kernel,
        in_specs=[VMEM, VMEM],
        out_specs=VMEM,
        out_shape=jax.ShapeDtypeStruct((here.shape[0], span), jnp.float32),
        compiler_params=params(),
        cost_estimate=pl.CostEstimate(flops=MEAN_FLOPS, bytes_accessed=12 * here.size, transcendentals=0),
        name="mean",
    )(here, there)


def finish(kernel, specs, args, down, up):
    return pl.pallas_call(
        kernel,
        in_specs=specs,
        out_specs=(VMEM, VMEM),
        out_shape=(
            jax.ShapeDtypeStruct(down.shape, jnp.float32),
            jax.ShapeDtypeStruct(up.shape, jnp.float32),
        ),
        compiler_params=params(),
        name="finish",
    )(*args)


def direct(bit, stored, window, sums, down, up, moved_up, product):
    kv = key_values(*product)
    moved = moved_columns(window, sums, 0, WINDOW, stored, moved_up)
    other = swap(moved, "rep", 1 << bit)
    return kv, *finish(direct_kernel, [SMEM] + [VMEM] * 2, (stored[0], moved, other), down, up)


def sliced(bit, span, stored, window, sums, down, up, moved_up, product):
    kv = key_values(*product)
    if span < WINDOW:
        moved = moved_columns(window, sums, 0, span)
        other = swap(moved, "rep", 1 << bit)
        later, _ = lax.optimization_barrier((sums[0], moved))
        far = moved_columns(
            window, (later, *sums[1:]), span, WINDOW - span, stored, moved_up, FAR_FLOPS
        )
        far_other = swap(far, "rep", 1 << bit)
        own = mean_of(moved, other, span)
    else:
        far = moved_columns(window, sums, 0, span, (), moved_up)
        far_other = swap(far, "rep", 1 << bit)
        own = mean_of(far, far_other, span)
    parts = [own] + [swap(own, "tp", mask) for mask in (4, 1, 3)]
    return kv, *finish(
        gather_kernel, [SMEM] + [VMEM] * 6, (stored[0], far, far_other, *parts), down, up
    )


def shards(
    tokens, key_value_weight, replica_down_maps, replica_up_maps, cotangent, optimizer_step_index
):
    rows, depth = tokens.shape[1:]
    rank, _, _, width = replica_up_maps.shape[1:]
    x = tokens[0]
    weight = key_value_weight.reshape(2 * depth, width)
    down = replica_down_maps.reshape(2 * rank, depth)
    up = replica_up_maps.reshape(2 * rank, width)
    cot = cotangent.reshape(2 * rows, width)
    step = optimizer_step_index
    bit_count = lax.axis_size("rep").bit_length() - 1
    which_bit = lax.rem(step, bit_count)[0]
    place = lax.axis_index("tp").reshape(1)

    stored = (x, weight, down)
    low, split, *held = low_grad(cot, up, *stored)
    from_z = swap(low, "tp", 4)
    held, sums = piece(0, stored, held)
    low = low + from_z
    from_y = swap(low, "tp", 1)
    held, sums = piece(1, stored, held, sums)
    low = low + from_y
    from_side = swap(low, "tp", 3)
    base, moved_up, turned, *window = last_piece(2, stored, held, sums, (place, step, up, split))

    branches = [
        functools.partial(direct, 0),
        functools.partial(sliced, 1, SPANS[1]),
        functools.partial(sliced, 2, SPANS[2]),
        functools.partial(sliced, 3, SPANS[3]),
        functools.partial(sliced, 4, SPANS[4]),
    ][:bit_count]
    kv, new_down, new_up = lax.switch(
        which_bit, branches, (place, x, down), window, (low, from_side, step), down, up, moved_up, (x, weight, base, turned, up)
    )
    return (
        kv.reshape(1, rows, 1, 2, width),
        new_down.reshape(replica_down_maps.shape),
        new_up.reshape(replica_up_maps.shape),
    )


def solution(mesh):
    placed = (
        P("rep", None, None),
        P(None, "tp", None, None),
        P("rep", None, None, None),
        P("rep", None, "tp", None, None),
        P("rep", None, "tp", None, None),
        P(),
    )
    return jax.shard_map(
        shards,
        mesh=mesh,
        in_specs=placed,
        out_specs=(
            P("rep", None, "tp", None, None),
            P("rep", None, None, None),
            P("rep", None, "tp", None, None),
        ),
        check_vma=False,
    )
```

```python
import functools

import jax
import jax.numpy as jnp
from jax import lax
from jax.experimental import pallas as pl
from jax.experimental.pallas import tpu as pltpu
from jax.sharding import PartitionSpec as P

SCALE = 0.5
PIECES = ((512,) * 5, (512,) * 5, (512,) * 6)
LATE = 0
AHEAD = (1, 1, 1)
GRAD_BLOCK = 512
LANES = 128
WINDOW = 2048
HELD_WINDOWS = 1
UP_COLUMNS = 128
SPANS = (0, 1408, 1408, 2048, 2048)
FAR_FLOPS = 1
MEAN_FLOPS = 40_000_000_000
NT = (((1,), (1,)), ((), ()))
HBM = pl.BlockSpec(memory_space=pltpu.HBM)
VMEM = pl.BlockSpec(memory_space=pltpu.VMEM)
SMEM = pl.BlockSpec(memory_space=pltpu.SMEM)


def params(mebibytes=20):
    return pltpu.CompilerParams(vmem_limit_bytes=mebibytes * 1024 * 1024)


def swap(value, axis, mask):
    pairs = [(source, source ^ mask) for source in range(lax.axis_size(axis))]
    return lax.ppermute(value, axis, pairs)


def rate_of(step_ref):
    step = jnp.full((1, 1), step_ref[0], jnp.int32).astype(jnp.float32)
    return 0.5 * (1.0 - 0.75 * step / 10000.0)


def label_of(place_ref):
    place = place_ref[0]
    z, b = place >> 2, (place >> 1) & 1
    a = (place & 1) ^ b
    return (z ^ a) * 2 + (z ^ b)


def every_other(ref, which, rows):
    return ref[pl.ds(which, rows, stride=2), :]


def in_hbm(*arrays):
    return [pltpu.with_memory_space_constraint(array, pltpu.HBM) for array in arrays]


def columns(ref, first, span):
    return ref.at[:, pl.ds(first, span)]


def span_copies(stored, targets, first, span, sems):
    x, weight, down = stored
    sources = (
        columns(x, first, span),
        None if weight is None else weight.at[pl.ds(2 * first, 2 * span)],
        None if down is None else columns(down, first, span),
    )
    return [
        pltpu.make_async_copy(source, target, sems.at[i])
        for i, (source, target) in enumerate(zip(sources, targets))
        if source is not None
    ]


def start_all(copies):
    for copy in copies:
        copy.start()


def wait_all(copies):
    for copy in copies:
        copy.wait()


def low_grad_kernel(
    cot_hbm, up_hbm, x_hbm, w_hbm, down_hbm,
    low_ref, split_ref, x_ref, w_ref, down_ref, cot_ref, up_ref, wide, sems, ahead_sems,
):
    rank = up_ref.shape[0] // 2
    parts, part_rows = cot_ref.shape[:2]
    rows = part_rows // 2
    up_copy = pltpu.make_async_copy(up_hbm, up_ref, sems.at[parts])
    copies = [
        pltpu.make_async_copy(
            cot_hbm.at[pl.ds(part * part_rows, part_rows)], cot_ref.at[part], sems.at[part]
        )
        for part in range(parts)
    ]
    start_all([up_copy, *copies])
    span = x_ref.shape[1]
    ahead = span_copies((x_hbm, w_hbm, down_hbm), (x_ref, w_ref, down_ref), 0, span, ahead_sems)
    start_all(ahead)
    up_copy.wait()
    ups = [every_other(up_ref, c, rank).astype(jnp.bfloat16) for c in range(2)]
    for part in range(parts):
        copies[part].wait()
        wide[...] = cot_ref[part].astype(jnp.float32)
        for c in range(2):
            cot = every_other(wide, c, rows).astype(jnp.bfloat16)
            split_ref[c, part * rows : (part + 1) * rows] = cot
            low_ref[c * rank : (c + 1) * rank, part * rows : (part + 1) * rows] = lax.dot_general(
                ups[c], cot, NT, preferred_element_type=jnp.float32
            )
    wait_all(ahead)


def ahead_span(index):
    return sum(PIECES[index][: AHEAD[index]])


def ahead_shapes(index, x, weight, down):
    span = ahead_span(index)
    return [
        jax.ShapeDtypeStruct((x.shape[0], span), x.dtype),
        jax.ShapeDtypeStruct((2 * span, weight.shape[1]), weight.dtype),
        jax.ShapeDtypeStruct((down.shape[0], span), down.dtype),
    ]


def low_grad(cot, up, x, weight, down):
    parts = 2
    rows, width = cot.shape[0] // 2, cot.shape[1]
    return pl.pallas_call(
        low_grad_kernel,
        in_specs=[HBM] * 5,
        out_specs=[VMEM] * 5,
        out_shape=(
            jax.ShapeDtypeStruct((up.shape[0], rows), jnp.float32),
            jax.ShapeDtypeStruct((2, rows, width), jnp.bfloat16),
            *ahead_shapes(0, x, weight, down),
        ),
        scratch_shapes=[
            pltpu.VMEM((parts, 2 * rows // parts, width), jnp.bfloat16),
            pltpu.VMEM(up.shape, jnp.float32),
            pltpu.VMEM((2 * rows // parts, width), jnp.float32),
            pltpu.SemaphoreType.DMA((parts + 1,)),
            pltpu.SemaphoreType.DMA((3,)),
        ],
        compiler_params=params(),
        name="low_grad",
    )(*in_hbm(cot, up, x, weight, down))


def accumulate(index, stored, held, base, low, buffers, sems):
    x_buf, w_buf, down_buf, wide = buffers
    begin, at, skipped = sum(sum(piece) for piece in PIECES[:index]), 0, 0
    late = len(PIECES[index]) - (LATE if index == len(PIECES) - 1 else 0)
    work = []
    for j, span in enumerate(PIECES[index]):
        ahead = held is not None and j < AHEAD[index]
        if low is None and j < late or ahead:
            skipped += span
        x_ref, w_ref, down_ref = held if ahead else (x_buf, w_buf, down_buf)
        here = at if ahead else at - skipped
        with_base = base is not None and (low is None or j < late)
        targets = (
            columns(x_ref, here, span),
            w_ref.at[pl.ds(2 * here, 2 * span)] if with_base else None,
            None if low is None else columns(down_ref, here, span),
        )
        x, weight, down = stored
        needed = (x, weight if with_base else None, down)
        if low is not None or j >= late:
            copies = [] if ahead else span_copies(needed, targets, begin + at, span, sems.at[j])
            start_all(copies)
            work.append((span, with_base, copies, targets))
        at += span

    def compute():
        for j, (span, with_base, copies, (x_ref, w_ref, down_ref)) in enumerate(work):
            wait_all(copies)
            x = x_ref[...]
            clear = index == 0 and j == 0
            if with_base:
                wide[: 2 * span] = w_ref[...].astype(jnp.float32)
                weight = jnp.concatenate(
                    [every_other(wide, c, span).astype(jnp.bfloat16) for c in range(2)], axis=1
                )
                base_part = jnp.dot(x, weight, preferred_element_type=jnp.float32)
                base[...] = base_part if clear else base[...] + base_part
            if low is not None:
                down = down_ref[...].astype(jnp.bfloat16)
                low_part = lax.dot_general(down, x, NT, preferred_element_type=jnp.float32)
                low[...] = low_part if clear else low[...] + low_part

    return begin + at, compute


def piece_kernel(index, *refs):
    stored, held, refs = refs[:3], refs[3:6], refs[6 if index == 0 else 8 :]
    base, low, *refs = refs
    targets, buffers, sems = refs[:3], refs[3:7], refs[7]
    end, compute = accumulate(index, stored, held, base, low, buffers, sems)
    ahead = span_copies(stored, targets, end, ahead_span(index + 1), sems.at[0])
    start_all(ahead)
    compute()
    wait_all(ahead)


def last_kernel(index, *refs):
    stored, held, refs = refs[:3], refs[3:6], refs[6:]
    _, low_in, place_ref, step_ref, up_ref, cot_ref, *refs = refs
    base, moved_ref, turned_ref, x_window, down_window, low, *buffers, sems = refs
    _, compute = accumulate(index, stored, held, base, low, buffers, sems)
    x_hbm, _, down_hbm = stored
    windows = x_hbm.shape[1] // WINDOW
    held_windows = []
    for n in range(HELD_WINDOWS):
        begin = pl.multiple_of(lax.rem(label_of(place_ref) + n, windows) * WINDOW, WINDOW)
        for i, (source, target) in enumerate(((x_hbm, x_window), (down_hbm, down_window))):
            copy = pltpu.make_async_copy(
                columns(source, begin, WINDOW),
                columns(target, n * WINDOW, WINDOW),
                sems.at[len(PIECES[index]) + n, i],
            )
            copy.start()
            held_windows.append(copy)
    low[...] = low_in[...]
    compute()
    rank = up_ref.shape[0] // 2
    factor = x_hbm.shape[1] ** (-0.5)
    turned = (factor * low[...]).astype(jnp.bfloat16)
    turned_ref[...] = turned
    rate = rate_of(step_ref)
    for c in range(2):
        grad = SCALE * jnp.dot(
            turned[c * rank : (c + 1) * rank], cot_ref[c], preferred_element_type=jnp.float32
        )
        moved_ref[c * rank : (c + 1) * rank, :] = every_other(up_ref, c, rank) - rate * grad
    wait_all(held_windows)


def kv_kernel(index, x_hbm, w_hbm, base_in, turned_ref, up_ref, kv_ref, base, pair, *refs):
    x_buf, w_buf, wide, out, sems = refs
    _, compute = accumulate(
        index, (x_hbm, w_hbm, None), None, base, None, (x_buf, w_buf, None, wide), sems
    )
    rows, width = kv_ref.shape[0] // 2, kv_ref.shape[1]
    rank = up_ref.shape[0] // 2
    ups = [every_other(up_ref, c, rank) for c in range(2)]
    none = jnp.zeros((rank, width), jnp.float32)
    both = jnp.concatenate(
        [
            jnp.concatenate([ups[0], none], axis=1),
            jnp.concatenate([none, ups[1]], axis=1),
        ],
        axis=0,
    ).astype(jnp.bfloat16)
    extra = jnp.dot(turned_ref[...].T, both, preferred_element_type=jnp.float32)
    base[...] = base_in[...] + SCALE * extra
    if LATE:
        compute()
    for c in range(2):
        pair[pl.ds(c, rows, stride=2), :] = base[:, c * width : (c + 1) * width]
    out[...] = pair[...].astype(jnp.bfloat16)
    copy = pltpu.make_async_copy(out, kv_ref, sems.at[0, 0])
    copy.start()
    copy.wait()


def key_values(x, weight, base, turned, up):
    rows, width = x.shape[0], weight.shape[1]
    index = len(PIECES) - 1
    span = max(sum(PIECES[index][len(PIECES[index]) - LATE :]), 128)
    return pl.pallas_call(
        functools.partial(kv_kernel, index),
        in_specs=[HBM] * 2 + [VMEM] * 3,
        out_specs=HBM,
        out_shape=pltpu.HBM((2 * rows, width), jnp.bfloat16),
        scratch_shapes=[
            pltpu.VMEM(base.shape, base.dtype),
            pltpu.VMEM((2 * rows, width), jnp.float32),
            pltpu.VMEM((rows, span), x.dtype),
            pltpu.VMEM((2 * span, width), weight.dtype),
            pltpu.VMEM((2 * max(PIECES[index]), width), jnp.float32),
            pltpu.VMEM((2 * rows, width), jnp.bfloat16),
            pltpu.SemaphoreType.DMA((len(PIECES[index]), 3)),
        ],
        compiler_params=params(),
        cost_estimate=pl.CostEstimate(
            flops=2 * rows * span * 4 * width, bytes_accessed=2 * span * (rows + 2 * width), transcendentals=0
        ),
        name="key_values",
    )(*in_hbm(x, weight), base, turned, up)


def last_piece(index, stored, held, sums, last):
    x, weight, down = stored
    base, low = sums
    rows, width, ranks = x.shape[0], weight.shape[1], down.shape[0]
    span = sum(PIECES[index])
    rest = span - ahead_span(index)
    return pl.pallas_call(
        functools.partial(last_kernel, index),
        in_specs=[HBM] * 3 + [VMEM] * 5 + [SMEM, SMEM, VMEM, VMEM],
        out_specs=[VMEM] * 5,
        input_output_aliases={6: 0},
        out_shape=[
            jax.ShapeDtypeStruct(base.shape, base.dtype),
            jax.ShapeDtypeStruct(last[2].shape, jnp.float32),
            jax.ShapeDtypeStruct(low.shape, jnp.bfloat16),
            jax.ShapeDtypeStruct((rows, HELD_WINDOWS * WINDOW), x.dtype),
            jax.ShapeDtypeStruct((ranks, HELD_WINDOWS * WINDOW), down.dtype),
        ],
        scratch_shapes=[
            pltpu.VMEM(low.shape, low.dtype),
            pltpu.VMEM((rows, rest), x.dtype),
            pltpu.VMEM((2 * rest, width), weight.dtype),
            pltpu.VMEM((ranks, rest), down.dtype),
            pltpu.VMEM((2 * max(PIECES[index]), width), jnp.float32),
            pltpu.SemaphoreType.DMA((len(PIECES[index]) + HELD_WINDOWS, 3)),
        ],
        compiler_params=params(),
        cost_estimate=pl.CostEstimate(
            flops=2 * rows * span * 512, bytes_accessed=2 * span * rows, transcendentals=0
        ),
        name="last_piece",
    )(*in_hbm(*stored), *held, *sums, *last)


def piece(index, stored, held, sums=()):
    x, weight, down = stored
    rows, width, ranks = x.shape[0], weight.shape[1], down.shape[0]
    totals = [
        jax.ShapeDtypeStruct((rows, 2 * width), jnp.float32),
        jax.ShapeDtypeStruct((ranks, rows), jnp.float32),
    ]
    span = sum(PIECES[index])
    rest = span - ahead_span(index)
    scratch = [
        pltpu.VMEM((rows, rest), x.dtype),
        pltpu.VMEM((2 * rest, width), weight.dtype),
        pltpu.VMEM((ranks, rest), down.dtype),
        pltpu.VMEM((2 * max(PIECES[index]), width), jnp.float32),
        pltpu.SemaphoreType.DMA((len(PIECES[index]), 3)),
    ]
    in_specs = [HBM] * 3 + [VMEM] * (3 + len(sums))
    kernel = functools.partial(piece_kernel, index)
    outs = totals + ahead_shapes(index + 1, *stored)
    aliases = {6: 0, 7: 1} if sums else {}
    out = pl.pallas_call(
        kernel,
        in_specs=in_specs,
        out_specs=[VMEM] * len(outs),
        out_shape=outs,
        scratch_shapes=scratch,
        input_output_aliases=aliases,
        compiler_params=params(),
        cost_estimate=pl.CostEstimate(
            flops=2 * rows * span * 4 * width,
            bytes_accessed=2 * span * (rows + 2 * width),
            transcendentals=0,
        ),
        name="piece",
    )(*in_hbm(*stored), *held, *sums)
    return out[2:], out[:2]


def moved_kernel(at, span, others, with_up, *refs):
    refs = list(refs)
    x_window, down_window, here, there, step_ref = refs[:5]
    refs = refs[5:]
    up_ref = refs.pop(0) if with_up else None
    block = span if span < 2 * GRAD_BLOCK else GRAD_BLOCK
    work = [
        (columns(x_window, n * WINDOW + at, span), columns(down_window, n * WINDOW + at, span), ())
        for n in range(HELD_WINDOWS if others else 1)
    ]
    if others:
        place_ref, x_hbm, down_hbm, out, x_buf, down_buf, sems = refs
        windows = x_hbm.shape[1] // WINDOW
        for i in range(HELD_WINDOWS, windows):
            window = lax.rem(label_of(place_ref) + i, windows)
            for j in range(span // block):
                n = (i - HELD_WINDOWS) * (span // block) + j
                source = pl.multiple_of(window * WINDOW + at + j * block, LANES)
                targets = [columns(buf, n * block, block) for buf in (x_buf, down_buf)]
                copies = [
                    pltpu.make_async_copy(columns(x_hbm, source, block), targets[0], sems.at[n, 0]),
                    pltpu.make_async_copy(columns(down_hbm, source, block), targets[1], sems.at[n, 1]),
                ]
                start_all(copies)
                work.append((*targets, copies))
    else:
        (out,) = refs
    factor = (4 * WINDOW) ** (-0.5)
    rate = rate_of(step_ref)
    grad_low = (SCALE * (here[...] + there[...])).astype(jnp.bfloat16)
    place = 0
    for x_ref, down_ref, copies in work:
        wait_all(copies)
        grad = factor * jnp.dot(grad_low, x_ref[...], preferred_element_type=jnp.float32)
        width = x_ref.shape[1]
        out[:, place : place + width] = down_ref[...] - rate * grad
        place += width
    if with_up:
        out[:, place:] = up_ref[...]


def moved_columns(window, sums, at, span, stored=(), up=None, flops=1):
    (x, down), (here, there, step) = window, sums
    rows, ranks = x.shape[0], down.shape[0]
    block = span if span < 2 * GRAD_BLOCK else GRAD_BLOCK
    in_specs, args = [VMEM] * 4 + [SMEM], [x, down, here, there, step]
    if up is not None:
        in_specs += [VMEM]
        args += [up]
    scratch, total = [], span
    if stored:
        place, x_all, down_all = stored
        total = span * (x_all.shape[1] // WINDOW)
        in_specs += [SMEM, HBM, HBM]
        args += [place, *in_hbm(x_all, down_all)]
        rest = total - HELD_WINDOWS * span
        scratch = [
            pltpu.VMEM((rows, rest), x.dtype),
            pltpu.VMEM((ranks, rest), down.dtype),
            pltpu.SemaphoreType.DMA((rest // block, 2)),
        ]
    return pl.pallas_call(
        functools.partial(moved_kernel, at, span, bool(stored), up is not None),
        in_specs=in_specs,
        out_specs=VMEM,
        out_shape=jax.ShapeDtypeStruct((ranks, total + (0 if up is None else UP_COLUMNS)), jnp.float32),
        scratch_shapes=scratch,
        compiler_params=params(),
        cost_estimate=pl.CostEstimate(
            flops=8 * rows * ranks * total * flops, bytes_accessed=2 * rows * total, transcendentals=0
        ),
        name="moved",
    )(*args)


def store_up(here, there, new_up):
    rank = new_up.shape[0] // 2
    mean = 0.5 * (here + there)
    for c in range(2):
        new_up[pl.ds(c, rank, stride=2), :] = mean[c * rank : (c + 1) * rank]


def store_others(place_ref, here, there, at, span, new_down):
    windows = new_down.shape[1] // WINDOW
    for i in range(windows):
        window = lax.rem(label_of(place_ref) + i, windows)
        begin = pl.multiple_of(window * WINDOW + at, LANES)
        part = slice(i * span, (i + 1) * span)
        new_down[:, pl.ds(begin, span)] = 0.5 * (here[:, part] + there[:, part])


def direct_kernel(place_ref, here, there, new_down, new_up):
    store_others(place_ref, here, there, 0, WINDOW, new_down)
    span = new_down.shape[1]
    store_up(here[:, span:], there[:, span:], new_up)


def gather_kernel(place_ref, here, there, own, from_z, from_y, from_side, new_down, new_up):
    span = own.shape[1]
    for mask, part in ((0, own), (3, from_z), (2, from_y), (1, from_side)):
        begin = pl.multiple_of((label_of(place_ref) ^ mask) * WINDOW, WINDOW)
        new_down[:, pl.ds(begin, span)] = part[...]
    if span < WINDOW:
        store_others(place_ref, here, there, span, WINDOW - span, new_down)
    at = here.shape[1] - UP_COLUMNS
    store_up(here[:, at:], there[:, at:], new_up)


def mean_kernel(here, there, mean):
    span = mean.shape[1]
    mean[...] = 0.5 * (here[:, :span] + there[:, :span])


def mean_of(here, there, span):
    return pl.pallas_call(
        mean_kernel,
        in_specs=[VMEM, VMEM],
        out_specs=VMEM,
        out_shape=jax.ShapeDtypeStruct((here.shape[0], span), jnp.float32),
        compiler_params=params(),
        cost_estimate=pl.CostEstimate(flops=MEAN_FLOPS, bytes_accessed=12 * here.size, transcendentals=0),
        name="mean",
    )(here, there)


def finish(kernel, specs, args, down, up):
    return pl.pallas_call(
        kernel,
        in_specs=specs,
        out_specs=(VMEM, VMEM),
        out_shape=(
            jax.ShapeDtypeStruct(down.shape, jnp.float32),
            jax.ShapeDtypeStruct(up.shape, jnp.float32),
        ),
        compiler_params=params(),
        name="finish",
    )(*args)


def direct(bit, stored, window, sums, down, up, moved_up, product):
    kv = key_values(*product)
    moved = moved_columns(window, sums, 0, WINDOW, stored, moved_up)
    other = swap(moved, "rep", 1 << bit)
    return kv, *finish(direct_kernel, [SMEM] + [VMEM] * 2, (stored[0], moved, other), down, up)


def sliced(bit, span, stored, window, sums, down, up, moved_up, product):
    kv = key_values(*product)
    if span < WINDOW:
        moved = moved_columns(window, sums, 0, span)
        other = swap(moved, "rep", 1 << bit)
        later, _ = lax.optimization_barrier((sums[0], moved))
        far = moved_columns(
            window, (later, *sums[1:]), span, WINDOW - span, stored, moved_up, FAR_FLOPS
        )
        far_other = swap(far, "rep", 1 << bit)
        own = mean_of(moved, other, span)
    else:
        far = moved_columns(window, sums, 0, span, (), moved_up)
        far_other = swap(far, "rep", 1 << bit)
        own = mean_of(far, far_other, span)
    parts = [own] + [swap(own, "tp", mask) for mask in (4, 1, 3)]
    return kv, *finish(
        gather_kernel, [SMEM] + [VMEM] * 6, (stored[0], far, far_other, *parts), down, up
    )


def shards(
    tokens, key_value_weight, replica_down_maps, replica_up_maps, cotangent, optimizer_step_index
):
    rows, depth = tokens.shape[1:]
    rank, _, _, width = replica_up_maps.shape[1:]
    x = tokens[0]
    weight = key_value_weight.reshape(2 * depth, width)
    down = replica_down_maps.reshape(2 * rank, depth)
    up = replica_up_maps.reshape(2 * rank, width)
    cot = cotangent.reshape(2 * rows, width)
    step = optimizer_step_index
    bit_count = lax.axis_size("rep").bit_length() - 1
    which_bit = lax.rem(step, bit_count)[0]
    place = lax.axis_index("tp").reshape(1)

    stored = (x, weight, down)
    low, split, *held = low_grad(cot, up, *stored)
    from_z = swap(low, "tp", 4)
    held, sums = piece(0, stored, held)
    low = low + from_z
    from_y = swap(low, "tp", 1)
    held, sums = piece(1, stored, held, sums)
    low = low + from_y
    from_side = swap(low, "tp", 3)
    base, moved_up, turned, *window = last_piece(2, stored, held, sums, (place, step, up, split))

    branches = [
        functools.partial(direct, 0),
        functools.partial(sliced, 1, SPANS[1]),
        functools.partial(sliced, 2, SPANS[2]),
        functools.partial(sliced, 3, SPANS[3]),
        functools.partial(sliced, 4, SPANS[4]),
    ][:bit_count]
    kv, new_down, new_up = lax.switch(
        which_bit, branches, (place, x, down), window, (low, from_side, step), down, up, moved_up, (x, weight, base, turned, up)
    )
    return (
        kv.reshape(1, rows, 1, 2, width),
        new_down.reshape(replica_down_maps.shape),
        new_up.reshape(replica_up_maps.shape),
    )


def solution(mesh):
    placed = (
        P("rep", None, None),
        P(None, "tp", None, None),
        P("rep", None, None, None),
        P("rep", None, "tp", None, None),
        P("rep", None, "tp", None, None),
        P(),
    )
    return jax.shard_map(
        shards,
        mesh=mesh,
        in_specs=placed,
        out_specs=(
            P("rep", None, "tp", None, None),
            P("rep", None, None, None),
            P("rep", None, "tp", None, None),
        ),
        check_vma=False,
    )
```
